128 devices in a mesh: dp: 16 (over y, x_lo, core), mp: 8 (over x_hi, z).
Axes of the slice: x: 4 (x_hi: 2, x_lo: 2; x = x_hi * 2 + x_lo), y: 4, z: 4, core: 2. Of those that a mesh axis runs over, the one named last changes fastest.
Arguments:
- grads: bfloat16 [256, 2048, 512], P('dp', 'mp'), may hold values from -6 to 6
- old_stat: float32 [256, 512, 512], P(('dp', 'mp')), may hold values from -0.015 to 64, as said below
- counts: int32 [256], P(('dp', 'mp')), may hold values from 2 to 6, as said below
Outputs:
- new_stat: float32 [256, 512, 512], P(('dp', 'mp'))
- roots: bfloat16 [256, 512, 512], P(None, 'mp')
The draws below stay inside these ranges and needn't reach their ends.
Inputs may be any that keep to these rules, and one draw needn't show every extreme that they name: old_stat is symmetric; each block's diagonal exceeds the sum of magnitudes of its row's other entries. `counts`: at least one block takes 6 iterations.
All inputs are finite; a program needn't handle non-finite values.
Results may differ from the reference program's by a relative error of at most 0.012.
Values may be sent and summed in bfloat16 or wider, within the bound.
A program may use at most 192 MiB of HBM per device.

```python
import jax
import jax.numpy as jnp
from jax import lax

BS = 512
ITERS = 6
NB = 256
ROWS = 2048


def draw_old_stat(key, part):
    key = jax.random.fold_in(key, 11)
    key_off, key_diag = jax.random.split(key)
    raw = jax.random.uniform(key_off, (NB, BS, BS), jnp.float32, -0.015, 0.015)
    sym = 0.5 * (raw + jnp.swapaxes(raw, 1, 2))
    eye = jnp.eye(BS, dtype=jnp.float32)
    diag = jnp.exp(jax.random.uniform(key_diag, (NB, BS), jnp.float32, jnp.log(8.0), jnp.log(64.0)))
    return sym * (1.0 - eye) + diag[:, :, None] * eye


def draw_counts(key, part):
    key = jax.random.fold_in(key, 23)
    key_vals, key_pos = jax.random.split(key)
    vals = jax.random.randint(key_vals, (NB,), 2, ITERS + 1)
    where = jax.random.randint(key_pos, (), 0, NB)
    return vals.at[where].set(ITERS).astype(jnp.int32)


def spiked(entries, rng, source, target, blocks, factor):
    def block_of(position):
        return (jnp.arange(entries.shape[position]) // (entries.shape[position] // blocks)).reshape((-1,) + (1,) * (entries.ndim - 1 - position))

    one_side = jax.random.permutation(rng, blocks)[block_of(target)]
    other_side = (block_of(target) + blocks // 2) % blocks
    return jnp.where((block_of(source) == one_side) | (block_of(source) == other_side), factor * entries, entries)


def level_of(own_key, dims, cuts, least, high):
    level, own = 1.0, jax.random.fold_in(own_key, 6)
    for axis_at, parts in cuts:
        heights = jnp.exp(jax.random.uniform(jax.random.fold_in(own, axis_at), (parts,), jnp.float32, least / len(cuts), high / len(cuts)))
        level = level * jnp.repeat(heights, dims[axis_at] // parts).reshape([-1 if axis == axis_at else 1 for axis in range(len(dims))])
    return level


def bell_draw_with(own_key, extent, spread, most, cuts, heavy, held_as=jnp.bfloat16):
    entries = spread * jax.random.normal(own_key, extent, jnp.float32)
    if cuts:
        entries = entries * level_of(own_key, extent, cuts, -0.22, 0.18)
    return jnp.clip(spiked(entries, jax.random.fold_in(own_key, 3), *heavy), -most, most).astype(held_as)


def setup_inputs(seed: int = 0) -> dict:
    seeds = jax.random.split(jax.random.key(seed), 4)
    return {
        "grads": bell_draw_with(seeds[0], (NB, ROWS, BS), 1.0, 6.0, ((0, 16), (1, 8)), (1, 0, 16, 2.0)),
        "old_stat": draw_old_stat(jax.random.fold_in(seeds[3], 71), 0),
        "counts": draw_counts(jax.random.fold_in(seeds[3], 71), 0),
    }


def newton_root(stat, count):
    eye = jnp.eye(BS, dtype=jnp.float32)
    norm = jnp.sqrt(jnp.sum(stat * stat))
    zval = 2.5 / norm
    mat_m = stat * zval
    mat_h = eye * jnp.sqrt(jnp.sqrt(zval))
    for step in range(ITERS):
        factor = 1.25 * eye - 0.25 * mat_m
        new_h = jnp.dot(mat_h, factor, precision=lax.Precision.HIGHEST)
        square = jnp.dot(factor, factor, precision=lax.Precision.HIGHEST)
        fourth = jnp.dot(square, square, precision=lax.Precision.HIGHEST)
        new_m = jnp.dot(fourth, mat_m, precision=lax.Precision.HIGHEST)
        live = step < count
        mat_h = jnp.where(live, new_h, mat_h)
        mat_m = jnp.where(live, new_m, mat_m)
    return mat_h.astype(jnp.bfloat16)

def one_block(items):
    grad_block, old_block, count = items
    gram = jnp.dot(grad_block.T, grad_block, preferred_element_type=jnp.float32)
    stat = 0.95 * old_block + 0.05 * gram
    return (stat, newton_root(stat, count))

def reference(grads, old_stat, counts):
    new_stat, roots = lax.map(one_block, (grads, old_stat, counts))
    return (new_stat, roots)
```

```python
import functools

import jax
import jax.numpy as jnp
from jax import lax
from jax.experimental import pallas as pl
from jax.experimental.pallas import tpu as pltpu
from jax.sharding import PartitionSpec as P

MESH = pl.DeviceIdType.MESH
F32, BF16 = jnp.float32, jnp.bfloat16
ITERS = 6
NY, NX, NC, NP = 4, 2, 2, 8
C0, C1, C2, C3, C4 = 1.25**4, -4 * 1.25**3 * 0.25, 6 * 1.25**2 * 0.25**2, -4 * 1.25 * 0.25**3, 0.25**4


def dot(left, right):
    return jnp.dot(left, right, preferred_element_type=F32)


def kernel(grads, old_hbm, counts, stat, out, got, old, root, mat, mat_b, sq_b, mix_b, mat_h, acc, sems):
    order = old.shape[1]
    dp, mp = lax.axis_index("dp"), lax.axis_index("mp")
    rows = grads.shape[1]
    slab = order // NP
    chunk = order // 2
    parts = [slice(r, r + chunk) for r in range(0, order, chunk)]

    across = (dp ^ 2, mp)
    up = (lax.rem(dp + 4, NY * NX * NC), mp)
    down = (lax.rem(dp + 12, NY * NX * NC), mp)
    sibling = (dp ^ 1, mp)
    peers = [(dp, mp ^ p) for p in range(NP)]

    barrier = pltpu.get_barrier_semaphore()
    partners = peers[1:] + [across, up, down, sibling]
    for partner in partners:
        pl.semaphore_signal(barrier, inc=1, device_id=partner, device_id_type=MESH)

    keep = [pltpu.make_async_copy(old_hbm.at[j], old.at[j], sems["old"].at[j]) for j in range(2)]
    for copy in keep:
        copy.start()
    mine = [
        pltpu.make_async_copy(
            grads.at[2 * mp + j], got.at[j, pl.ds(mp * rows, rows)], sems["mine"].at[j]
        )
        for j in range(2)
    ]
    for copy in mine:
        copy.start()
    pl.semaphore_wait(barrier, len(partners))

    def grad_copy(j, p):
        return pltpu.make_async_remote_copy(
            src_ref=grads.at[2 * (mp ^ p) + j],
            dst_ref=got.at[j, pl.ds(mp * rows, rows)],
            send_sem=sems["gsend"].at[j, p],
            recv_sem=sems["grecv"].at[j, p],
            device_id=peers[p],
            device_id_type=MESH,
        )

    grad_copies = [[p and grad_copy(j, p) for p in range(NP)] for j in range(2)]

    def add_gram(j, p):
        block = got[j, pl.ds(pl.multiple_of((mp ^ p) * rows, rows), rows), :]
        gram = lax.dot_general(block, block, (((0,), (0,)), ((), ())), preferred_element_type=F32)
        if p == 0:
            acc[...] = gram
        else:
            acc[...] += gram

    def update_stat(j):
        keep[j].wait()
        total = jnp.zeros((1, order), F32)
        for r in parts:
            new = 0.95 * old[j, r, :] + 0.05 * acc[r, :]
            stat[j, r, :] = new
            total = total + jnp.sum(new * new, axis=0, keepdims=True)
        total = jnp.sum(total, axis=1, keepdims=True)
        zval = 2.5 / jnp.sqrt(total)
        start = jnp.sqrt(jnp.sqrt(zval))
        for r in parts:
            scaled = stat[j, r, :] * zval
            mat[r, :] = scaled
            mat_b[r, :] = scaled.astype(BF16)
            row = lax.broadcasted_iota(jnp.int32, (chunk, order), 0) + r.start
            col = lax.broadcasted_iota(jnp.int32, (chunk, order), 1)
            mat_h[r, :] = start * (jnp.where(row == col, 1.25, 0.0) - 0.25 * scaled)

    def step_m():
        for r in parts:
            square = dot(mat_b[r, :], mat_b[...])
            sq_b[r, :] = square.astype(BF16)
            mat[r, :] = C0 * mat[r, :] + C1 * square
        for r in parts:
            cube = dot(mat_b[r, :], sq_b[...])
            mat[r, :] = mat[r, :] + C2 * cube
            mix_b[r, :] = (C3 * sq_b[r, :].astype(F32) + C4 * cube).astype(BF16)
        for r in parts:
            new = mat[r, :] + dot(sq_b[r, :], mix_b[...])
            mat[r, :] = new
            mat_b[r, :] = new.astype(BF16)

    def step_h(j, it):
        share = jnp.where(it < counts[j], 0.25, 0.0).astype(F32)
        for r in parts:
            held = mat_h[r, :]
            mat_h[r, :] = held + share * (held - dot(held.astype(BF16), mat_b[...]))

    def finish(j):
        share = jnp.where(ITERS - 1 < counts[j], 0.25, 0.0).astype(F32)
        for r in parts:
            held = mat_h[r, :]
            held = held + share * (held - dot(held.astype(BF16), mat_b[...]))
            root[j, r, :] = held.astype(BF16)

    def slab_copy(j, p):
        return pltpu.make_async_remote_copy(
            src_ref=root.at[j, pl.ds(pl.multiple_of((mp ^ p) * slab, slab), slab)],
            dst_ref=out.at[dp, mp, j],
            send_sem=sems["ssend"].at[j, p],
            recv_sem=sems["srecv"].at[j, p],
            device_id=peers[p],
            device_id_type=MESH,
        )

    slab_copies = [[p and slab_copy(j, p) for p in range(NP)] for j in range(2)]

    def piece(j, dy, dx, t):
        origin = lax.rem(dp + 4 * (NY - dy), NY * NX * NC) ^ (2 * dx)
        return out.at[origin, pl.ds(2 * ((mp // 2) ^ t), 2), j]

    def move(j, dy, dx, t, way):
        target = {"x": across, "+": up, "-": down, "s": sibling}[way]
        to_dy = {"x": dy, "+": (dy + 1) % NY, "-": (dy - 1) % NY, "s": dy}[way]
        to_dx = dx ^ 1 if way == "x" else dx
        side = "xys"["x+-s".index(way) if way == "x" else (2 if way == "s" else 1)]
        name = {"x": 0, "y": 0, "s": 1}[side]
        return pltpu.make_async_remote_copy(
            src_ref=piece(j, dy, dx, t),
            dst_ref=piece(j, dy, dx, t),
            send_sem=sems["bsend"].at[j, "x+-s".index(way), dy * 2 + dx, t],
            recv_sem=sems["brecv"].at[j, name, to_dy * 2 + to_dx, t],
            device_id=target,
            device_id_type=MESH,
        )

    started = []

    def send(j, dy, dx, t, ways):
        for way in ways:
            copy = move(j, dy, dx, t, way)
            copy.start()
            started.append(copy)

    def arrived(j, dy, dx, t, side=0):
        pltpu.make_async_remote_copy(
            src_ref=piece(j, dy, dx, t),
            dst_ref=piece(j, dy, dx, t),
            send_sem=sems["bsend"].at[j, 3, dy * 2 + dx, t],
            recv_sem=sems["brecv"].at[j, side, dy * 2 + dx, t],
            device_id=sibling,
            device_id_type=MESH,
        ).wait_recv()

    def spread(j):
        for p in range(1, NP):
            slab_copies[j][p].start()
        out[dp, mp, j] = root[j, pl.ds(pl.multiple_of(mp * slab, slab), slab), :]
        for t in range(NP // 2):
            for p in (2 * t, 2 * t + 1):
                if p:
                    slab_copies[j][p].wait_recv()
            send(j, 0, 0, t, {0: "x+-s", 1: "x-+s", 2: "+-xs", 3: "-+xs"}[t])

    relays = [
        (0, 1, 0, "+-s"),
        (0, 1, 1, "-+s"),
        (1, 0, 0, "+s"),
        (3, 0, 1, "-s"),
        (1, 0, 2, "+xs"),
        (3, 0, 3, "-xs"),
        (3, 0, 2, "xs"),
        (1, 0, 3, "xs"),
        (1, 0, 1, "s"),
        (3, 0, 0, "s"),
        (0, 1, 2, "s"),
        (0, 1, 3, "s"),
        (1, 1, 0, "+s"),
        (3, 1, 1, "-s"),
        (1, 1, 1, "s"),
        (3, 1, 0, "s"),
        (2, 0, 2, "xs"),
        (2, 0, 3, "xs"),
        (2, 0, 0, "s"),
        (2, 0, 1, "s"),
        (1, 1, 2, "s"),
        (3, 1, 3, "s"),
        (3, 1, 2, "s"),
        (1, 1, 3, "s"),
        (2, 1, 0, "s"),
        (2, 1, 1, "s"),
        (2, 1, 2, "s"),
        (2, 1, 3, "s"),
    ]

    def relay(j, first, last):
        for dy, dx, t, ways in relays[first:last]:
            arrived(j, dy, dx, t)
            send(j, dy, dx, t, ways)

    for p in range(1, NP):
        grad_copies[0][p].start()
    mine[0].wait()
    add_gram(0, 0)
    for p in range(1, NP):
        grad_copies[0][p].wait_recv()
        add_gram(0, p)
        grad_copies[0][p].wait_send()
        grad_copies[1][p].start()
    update_stat(0)
    step_m()

    def body(it, _):
        step_h(0, it)
        step_m()
        return 0

    lax.fori_loop(1, ITERS - 1, body, 0)
    finish(0)
    spread(0)

    mine[1].wait()
    add_gram(1, 0)
    relay(0, 0, 2)
    for p in range(1, NP):
        grad_copies[1][p].wait_recv()
        add_gram(1, p)
        grad_copies[1][p].wait_send()
    update_stat(1)
    step_m()
    relay(0, 2, 4)
    stops = {1: (4, 8), 2: (8, 12), 3: (12, 16), 4: (16, 20)}
    for it in range(1, ITERS - 1):
        step_h(1, it)
        step_m()
        relay(0, *stops[it])
    finish(1)
    spread(1)
    relay(0, 20, len(relays))
    relay(1, 0, len(relays))

    for j in range(2):
        for dy in range(NY):
            for dx in range(NX):
                for t in range(4):
                    arrived(j, dy, dx, t, 1)
        for p in range(1, NP):
            slab_copies[j][p].wait_send()
    for copy in started:
        copy.wait_send()


def solution(mesh):
    def step(grads, old_stat, counts):
        order = old_stat.shape[1]
        rows = grads.shape[1]
        slab = order // NP
        square = (order, order)
        anywhere = pl.BlockSpec(memory_space=pl.ANY)
        sems = {
            "old": pltpu.SemaphoreType.DMA((2,)),
            "mine": pltpu.SemaphoreType.DMA((2,)),
            "gsend": pltpu.SemaphoreType.DMA((2, NP)),
            "grecv": pltpu.SemaphoreType.DMA((2, NP)),
            "ssend": pltpu.SemaphoreType.DMA((2, NP)),
            "srecv": pltpu.SemaphoreType.DMA((2, NP)),
            "bsend": pltpu.SemaphoreType.DMA((2, 4, NY * NX, 4)),
            "brecv": pltpu.SemaphoreType.DMA((2, 2, NY * NX, 4)),
        }
        stat, out = pl.pallas_call(
            kernel,
            out_shape=(
                pltpu.VMEM((2, order, order), F32),
                pltpu.VMEM((NY * NX * NC, NP, 2, slab, order), BF16),
            ),
            in_specs=[anywhere, anywhere, pl.BlockSpec(memory_space=pltpu.SMEM)],
            out_specs=(pl.BlockSpec(memory_space=pltpu.VMEM), pl.BlockSpec(memory_space=pltpu.VMEM)),
            scratch_shapes=[
                pltpu.VMEM((2, NP * rows, order), BF16),
                pltpu.VMEM((2, order, order), F32),
                pltpu.VMEM((2, order, order), BF16),
                pltpu.VMEM(square, F32),
                pltpu.VMEM(square, BF16),
                pltpu.VMEM(square, BF16),
                pltpu.VMEM(square, BF16),
                pltpu.VMEM(square, F32),
                pltpu.VMEM(square, F32),
                sems,
            ],
            name="shampoo_roots",
            compiler_params=pltpu.CompilerParams(
                collective_id=0, has_side_effects=True, vmem_limit_bytes=24 * 2**20
            ),
        )(grads, old_stat, counts)
        return stat, out.reshape(NY * NX * NC * NP * 2, slab, order)

    return jax.shard_map(
        step,
        mesh=mesh,
        in_specs=(P("dp", "mp", None), P(("dp", "mp"), None, None), P(("dp", "mp"))),
        out_specs=(P(("dp", "mp"), None, None), P(None, "mp", None)),
        check_vma=False,
    )
```

```python
import functools

import jax
import jax.numpy as jnp
from jax import lax
from jax.experimental import pallas as pl
from jax.experimental.pallas import tpu as pltpu
from jax.sharding import PartitionSpec as P

MESH = pl.DeviceIdType.MESH
F32, BF16 = jnp.float32, jnp.bfloat16
ITERS = 6
NY, NX, NC, NP = 4, 2, 2, 8
C0, C1, C2, C3, C4 = 1.25**4, -4 * 1.25**3 * 0.25, 6 * 1.25**2 * 0.25**2, -4 * 1.25 * 0.25**3, 0.25**4


STORES = 8
X, Y = "x", "y"
MOST = ((X, "-"), (X, "+"), (X, "-"), (Y, "+"))
HALF = ((X, "+"), (X, "-"), (Y, "+"), (Y, "-"))
KINDS = (MOST, HALF)
STOPS = (4, 12, 15, 18, 21, 24, 28)


def ways_on(kind, dy, dx):
    first, far = kind
    near = "-" if far == "+" else "+"
    ways = ""
    if first == "x" and (dy, dx) == (0, 0):
        ways += "x"
    if first == "x" or dx == 0:
        if dy == 0:
            ways += far + near
        elif dy == (1 if far == "+" else NY - 1):
            ways += far
    if first == "y" and dx == 0:
        ways += "x"
    return ways


def arrival_order(kinds):
    free = {"x": 0.0, "+": 0.0, "-": 0.0}
    events = [(0.6 * t, 0, 0, t) for t in range(len(kinds))]
    order = []
    while events:
        events.sort()
        now, dy, dx, t = events.pop(0)
        if (dy, dx) != (0, 0):
            order.append((dy, dx, t))
        for way in ways_on(kinds[t], dy, dx):
            free[way] = max(free[way], now) + 1.0
            to_dy = (dy + {"x": 0, "+": 1, "-": -1}[way]) % NY
            events.append((free[way] + 1.0, to_dy, dx ^ 1 if way == "x" else dx, t))
    return order


def dot(left, right):
    return jnp.dot(left, right, preferred_element_type=F32)


def kernel(grads, old_hbm, counts_hbm, stat, out, counts, got, old, root, mat, mat_b, sq_b, mix_b, mat_h, acc, sems):
    order = old.shape[1]
    dp, mp = lax.axis_index("dp"), lax.axis_index("mp")
    rows = grads.shape[1]
    slab = order // NP
    chunk = order // 2
    parts = [slice(r, r + chunk) for r in range(0, order, chunk)]

    across = (dp ^ 2, mp)
    up = (lax.rem(dp + 4, NY * NX * NC), mp)
    down = (lax.rem(dp + 12, NY * NX * NC), mp)
    sibling = (dp ^ 1, mp)
    peers = [(dp, mp ^ p) for p in range(NP)]

    barrier = pltpu.get_barrier_semaphore()
    partners = peers[1:] + [across, up, down, sibling]
    for partner in partners:
        pl.semaphore_signal(barrier, inc=1, device_id=partner, device_id_type=MESH)

    keep = [pltpu.make_async_copy(old_hbm.at[j], old.at[j], sems["old"].at[j]) for j in range(2)]
    tally = pltpu.make_async_copy(counts_hbm, counts, sems["count"])
    tally.start()
    for copy in keep:
        copy.start()
    mine = [
        pltpu.make_async_copy(
            grads.at[2 * mp + j], got.at[j, pl.ds(mp * rows, rows)], sems["mine"].at[j]
        )
        for j in range(2)
    ]
    for copy in mine:
        copy.start()
    pl.semaphore_wait(barrier, len(partners))

    def grad_copy(j, p):
        return pltpu.make_async_remote_copy(
            src_ref=grads.at[2 * (mp ^ p) + j],
            dst_ref=got.at[j, pl.ds(mp * rows, rows)],
            send_sem=sems["gsend"].at[j, p],
            recv_sem=sems["grecv"].at[j, p],
            device_id=peers[p],
            device_id_type=MESH,
        )

    grad_copies = [[p and grad_copy(j, p) for p in range(NP)] for j in range(2)]

    def add_gram(j, p):
        block = got[j, pl.ds(pl.multiple_of((mp ^ p) * rows, rows), rows), :]
        gram = lax.dot_general(block, block, (((0,), (0,)), ((), ())), preferred_element_type=F32)
        if p == 0:
            acc[...] = gram
        else:
            acc[...] += gram

    def update_stat(j):
        keep[j].wait()
        total = jnp.zeros((1, order), F32)
        for r in parts:
            new = 0.95 * old[j, r, :] + 0.05 * acc[r, :]
            stat[j, r, :] = new
            total = total + jnp.sum(new * new, axis=0, keepdims=True)
        total = jnp.sum(total, axis=1, keepdims=True)
        zval = 2.5 / jnp.sqrt(total)
        start = jnp.sqrt(jnp.sqrt(zval))
        for r in parts:
            scaled = stat[j, r, :] * zval
            mat[r, :] = scaled
            mat_b[r, :] = scaled.astype(BF16)
            row = lax.broadcasted_iota(jnp.int32, (chunk, order), 0) + r.start
            col = lax.broadcasted_iota(jnp.int32, (chunk, order), 1)
            mat_h[r, :] = start * (jnp.where(row == col, 1.25, 0.0) - 0.25 * scaled)

    def step_m():
        for r in parts:
            square = dot(mat_b[r, :], mat_b[...])
            sq_b[r, :] = square.astype(BF16)
            mat[r, :] = C0 * mat[r, :] + C1 * square
        for r in parts:
            cube = dot(mat_b[r, :], sq_b[...])
            mat[r, :] = mat[r, :] + C2 * cube
            mix_b[r, :] = (C3 * sq_b[r, :].astype(F32) + C4 * cube).astype(BF16)
        for r in parts:
            new = mat[r, :] + dot(sq_b[r, :], mix_b[...])
            mat[r, :] = new
            mat_b[r, :] = new.astype(BF16)

    def step_h(j, it):
        share = jnp.where(it < counts[j], 0.25, 0.0).astype(F32)
        for r in parts:
            held = mat_h[r, :]
            mat_h[r, :] = held + share * (held - dot(held.astype(BF16), mat_b[...]))

    def finish(j):
        share = jnp.where(ITERS - 1 < counts[j], 0.25, 0.0).astype(F32)
        for r in parts:
            held = mat_h[r, :]
            held = held + share * (held - dot(held.astype(BF16), mat_b[...]))
            root[j, r, :] = held.astype(BF16)

    def slab_copy(j, p):
        return pltpu.make_async_remote_copy(
            src_ref=root.at[j, pl.ds(pl.multiple_of((mp ^ p) * slab, slab), slab)],
            dst_ref=out.at[dp, mp, j],
            send_sem=sems["ssend"].at[j, p],
            recv_sem=sems["srecv"].at[j, p],
            device_id=peers[p],
            device_id_type=MESH,
        )

    slab_copies = [[p and slab_copy(j, p) for p in range(NP)] for j in range(2)]

    def piece(j, dy, dx, t):
        origin = lax.rem(dp + 4 * (NY - dy), NY * NX * NC) ^ (2 * dx)
        return out.at[origin, pl.ds(2 * ((mp // 2) ^ t), 2), j]

    def move(j, dy, dx, t, way):
        target = {"x": across, "+": up, "-": down, "s": sibling}[way]
        to_dy = {"x": dy, "+": (dy + 1) % NY, "-": (dy - 1) % NY, "s": dy}[way]
        to_dx = dx ^ 1 if way == "x" else dx
        side = "xys"["x+-s".index(way) if way == "x" else (2 if way == "s" else 1)]
        name = {"x": 0, "y": 0, "s": 1}[side]
        return pltpu.make_async_remote_copy(
            src_ref=piece(j, dy, dx, t),
            dst_ref=piece(j, dy, dx, t),
            send_sem=sems["bsend"].at[j, "x+-s".index(way), dy * 2 + dx, t],
            recv_sem=sems["brecv"].at[j, name, to_dy * 2 + to_dx, t],
            device_id=target,
            device_id_type=MESH,
        )

    started = []

    def send(j, dy, dx, t, ways):
        for way in ways:
            copy = move(j, dy, dx, t, way)
            copy.start()
            started.append(copy)

    def arrived(j, dy, dx, t, side=0):
        pltpu.make_async_remote_copy(
            src_ref=piece(j, dy, dx, t),
            dst_ref=piece(j, dy, dx, t),
            send_sem=sems["bsend"].at[j, 3, dy * 2 + dx, t],
            recv_sem=sems["brecv"].at[j, side, dy * 2 + dx, t],
            device_id=sibling,
            device_id_type=MESH,
        ).wait_recv()

    def spread(j):
        for p in range(1, NP):
            slab_copies[j][p].start()
        out[dp, mp, j] = root[j, pl.ds(pl.multiple_of(mp * slab, slab), slab), :]
        for t in range(NP // 2):
            for p in (2 * t, 2 * t + 1):
                if p:
                    slab_copies[j][p].wait_recv()
            send(j, 0, 0, t, ways_on(KINDS[j][t], 0, 0) + "s")

    relays = [arrival_order(KINDS[j]) for j in range(2)]

    def relay(j, first, last):
        for dy, dx, t in relays[j][first:last]:
            arrived(j, dy, dx, t)
            send(j, dy, dx, t, ways_on(KINDS[j][t], dy, dx) + "s")

    core = lax.rem(dp, NC)

    def take_turn(p):
        pl.semaphore_wait(sems["turn"].at[p], 1)

    def pass_turn(p):
        pl.semaphore_signal(sems["turn"].at[p], inc=1, device_id=sibling, device_id_type=MESH)

    for p in range(1, NP):
        pl.when(core == 1)(functools.partial(take_turn, p))
        grad_copies[0][p].start()
    mine[0].wait()
    add_gram(0, 0)
    for p in range(1, NP):
        grad_copies[0][p].wait_send()
        pass_turn(p)
    for p in range(1, NP):
        grad_copies[0][p].wait_recv()
        add_gram(0, p)
    tally.wait()
    update_stat(0)
    step_m()

    def body(it, _):
        step_h(0, it)
        step_m()
        return 0

    lax.fori_loop(1, ITERS - 1, body, 0)
    finish(0)

    spread(0)
    for p in range(1, NP):
        pl.when(core == 0)(functools.partial(take_turn, p))
        grad_copies[1][p].start()

    relay(0, 0, STOPS[0])
    relay(0, STOPS[0], STOPS[1])
    mine[1].wait()
    add_gram(1, 0)
    for p in range(1, NP):
        grad_copies[1][p].wait_send()
    for p in range(1, NP):
        grad_copies[1][p].wait_recv()
        add_gram(1, p)
    update_stat(1)
    step_m()
    for it in range(1, ITERS - 1):
        relay(0, STOPS[it], STOPS[it + 1])
        step_h(1, it)
        step_m()
    relay(0, STOPS[ITERS - 1], STOPS[ITERS])
    finish(1)
    spread(1)
    relay(0, STOPS[ITERS], len(relays[0]))
    relay(1, 0, len(relays[1]))

    for j in range(2):
        for dy in range(NY):
            for dx in range(NX):
                for t in range(4):
                    arrived(j, dy, dx, t, 1)
        for p in range(1, NP):
            slab_copies[j][p].wait_send()
    for copy in started:
        copy.wait_send()


def store(stat, out, stat_to, out_to, sems):
    size = out.shape[0] // STORES
    copies = [pltpu.make_async_copy(stat, stat_to, sems.at[STORES])]
    for k in range(STORES):
        span = pl.ds(k * size, size)
        copies.append(pltpu.make_async_copy(out.at[span], out_to.at[span], sems.at[k]))
    for copy in copies:
        copy.start()
    for copy in copies:
        copy.wait()


def solution(mesh):
    def step(grads, old_stat, counts):
        order = old_stat.shape[1]
        rows = grads.shape[1]
        slab = order // NP
        square = (order, order)
        sems = {
            "old": pltpu.SemaphoreType.DMA((2,)),
            "mine": pltpu.SemaphoreType.DMA((2,)),
            "count": pltpu.SemaphoreType.DMA(()),
            "turn": pltpu.SemaphoreType.REGULAR((NP,)),
            "gsend": pltpu.SemaphoreType.DMA((2, NP)),
            "grecv": pltpu.SemaphoreType.DMA((2, NP)),
            "ssend": pltpu.SemaphoreType.DMA((2, NP)),
            "srecv": pltpu.SemaphoreType.DMA((2, NP)),
            "bsend": pltpu.SemaphoreType.DMA((2, 4, NY * NX, 4)),
            "brecv": pltpu.SemaphoreType.DMA((2, 2, NY * NX, 4)),
        }
        stat, out = pl.pallas_call(
            kernel,
            out_shape=(
                pltpu.VMEM((2, order, order), F32),
                pltpu.VMEM((NY * NX * NC, NP, 2, slab, order), BF16),
            ),
            in_specs=[pl.BlockSpec(memory_space=pltpu.HBM)] * 3,
            out_specs=(pl.BlockSpec(memory_space=pltpu.VMEM), pl.BlockSpec(memory_space=pltpu.VMEM)),
            scratch_shapes=[
                pltpu.SMEM((2,), jnp.int32),
                pltpu.VMEM((2, NP * rows, order), BF16),
                pltpu.VMEM((2, order, order), F32),
                pltpu.VMEM((2, order, order), BF16),
                pltpu.VMEM(square, F32),
                pltpu.VMEM(square, BF16),
                pltpu.VMEM(square, BF16),
                pltpu.VMEM(square, BF16),
                pltpu.VMEM(square, F32),
                pltpu.VMEM(square, F32),
                sems,
            ],
            name="shampoo_roots",
            compiler_params=pltpu.CompilerParams(
                collective_id=0, has_side_effects=True, vmem_limit_bytes=24 * 2**20
            ),
        )(*(pltpu.with_memory_space_constraint(x, pltpu.HBM) for x in (grads, old_stat, counts)))
        out = out.reshape(NY * NX * NC * NP * 2, slab, order)
        anywhere = pl.BlockSpec(memory_space=pl.ANY)
        return pl.pallas_call(
            store,
            out_shape=(pltpu.HBM(stat.shape, F32), pltpu.HBM(out.shape, BF16)),
            in_specs=[pl.BlockSpec(memory_space=pltpu.VMEM)] * 2,
            out_specs=(pl.BlockSpec(memory_space=pltpu.HBM),) * 2,
            scratch_shapes=[pltpu.SemaphoreType.DMA((STORES + 1,))],
            name="store_results",
            compiler_params=pltpu.CompilerParams(vmem_limit_bytes=2**20),
        )(*(pltpu.with_memory_space_constraint(x, pltpu.VMEM) for x in (stat, out)))

    return jax.shard_map(
        step,
        mesh=mesh,
        in_specs=(P("dp", "mp", None), P(("dp", "mp"), None, None), P(("dp", "mp"))),
        out_specs=(P(("dp", "mp"), None, None), P(None, "mp", None)),
        check_vma=False,
    )
```

```python
import functools

import jax
import jax.numpy as jnp
from jax import lax
from jax.experimental import pallas as pl
from jax.experimental.pallas import tpu as pltpu
from jax.sharding import PartitionSpec as P

MESH = pl.DeviceIdType.MESH
F32, BF16 = jnp.float32, jnp.bfloat16
ITERS = 6
NY, NX, NC, NP = 4, 2, 2, 8
C0, C1, C2, C3, C4 = 1.25**4, -4 * 1.25**3 * 0.25, 6 * 1.25**2 * 0.25**2, -4 * 1.25 * 0.25**3, 0.25**4


STORES = 8
X, Y = "x", "y"
FULL = ((X, "+"), (X, "-"), (X, "+"), (X, "-"))
HALF = ((Y, "+"), (X, "+"), (X, "-"), (Y, "-"))
KINDS = (FULL, HALF)
STOPS = (4, 10, 12, 14, 17, 20, 24)


def ways_on(kind, dy, dx):
    first, far = kind
    near = "-" if far == "+" else "+"
    ways = ""
    if first == "x" and (dy, dx) == (0, 0):
        ways += "x"
    if first == "x" or dx == 0:
        if dy == 0:
            ways += far + near
        elif dy == (1 if far == "+" else NY - 1):
            ways += far
    if first == "y" and dx == 0:
        ways += "x"
    return ways


def arrival_order(kinds):
    free = {"x": 0.0, "+": 0.0, "-": 0.0}
    events = [(0.6 * t, 0, 0, t) for t in range(len(kinds))]
    order = []
    while events:
        events.sort()
        now, dy, dx, t = events.pop(0)
        if (dy, dx) != (0, 0):
            order.append((dy, dx, t))
        for way in ways_on(kinds[t], dy, dx):
            free[way] = max(free[way], now) + 1.0
            to_dy = (dy + {"x": 0, "+": 1, "-": -1}[way]) % NY
            events.append((free[way] + 1.0, to_dy, dx ^ 1 if way == "x" else dx, t))
    return order


def dot(left, right):
    return jnp.dot(left, right, preferred_element_type=F32)


def kernel(grads, old_hbm, counts_hbm, stat, out, counts, got, old, root, mat, mat_b, sq_b, mix_b, mat_h, acc, sems):
    order = old.shape[1]
    dp, mp = lax.axis_index("dp"), lax.axis_index("mp")
    rows = grads.shape[1]
    slab = order // NP
    chunk = order // 2
    parts = [slice(r, r + chunk) for r in range(0, order, chunk)]

    across = (dp ^ 2, mp)
    up = (lax.rem(dp + 4, NY * NX * NC), mp)
    down = (lax.rem(dp + 12, NY * NX * NC), mp)
    sibling = (dp ^ 1, mp)
    peers = [(dp, mp ^ p) for p in range(NP)]

    barrier = pltpu.get_barrier_semaphore()
    partners = peers[1:] + [across, up, down, sibling]
    for partner in partners:
        pl.semaphore_signal(barrier, inc=1, device_id=partner, device_id_type=MESH)

    keep = [pltpu.make_async_copy(old_hbm.at[j], old.at[j], sems["old"].at[j]) for j in range(2)]
    tally = pltpu.make_async_copy(counts_hbm, counts, sems["count"])
    tally.start()
    for copy in keep:
        copy.start()
    mine = [
        pltpu.make_async_copy(
            grads.at[2 * mp + j], got.at[j, pl.ds(mp * rows, rows)], sems["mine"].at[j]
        )
        for j in range(2)
    ]
    for copy in mine:
        copy.start()
    pl.semaphore_wait(barrier, len(partners))

    def grad_copy(j, p):
        return pltpu.make_async_remote_copy(
            src_ref=grads.at[2 * (mp ^ p) + j],
            dst_ref=got.at[j, pl.ds(mp * rows, rows)],
            send_sem=sems["gsend"].at[j, p],
            recv_sem=sems["grecv"].at[j, p],
            device_id=peers[p],
            device_id_type=MESH,
        )

    grad_copies = [[p and grad_copy(j, p) for p in range(NP)] for j in range(2)]

    def add_gram(j, p):
        block = got[j, pl.ds(pl.multiple_of((mp ^ p) * rows, rows), rows), :]
        gram = lax.dot_general(block, block, (((0,), (0,)), ((), ())), preferred_element_type=F32)
        if p == 0:
            acc[...] = gram
        else:
            acc[...] += gram

    def update_stat(j):
        keep[j].wait()
        total = jnp.zeros((1, order), F32)
        for r in parts:
            new = 0.95 * old[j, r, :] + 0.05 * acc[r, :]
            stat[j, r, :] = new
            total = total + jnp.sum(new * new, axis=0, keepdims=True)
        total = jnp.sum(total, axis=1, keepdims=True)
        zval = 2.5 / jnp.sqrt(total)
        start = jnp.sqrt(jnp.sqrt(zval))
        for r in parts:
            scaled = stat[j, r, :] * zval
            mat[r, :] = scaled
            mat_b[r, :] = scaled.astype(BF16)
            row = lax.broadcasted_iota(jnp.int32, (chunk, order), 0) + r.start
            col = lax.broadcasted_iota(jnp.int32, (chunk, order), 1)
            mat_h[r, :] = start * (jnp.where(row == col, 1.25, 0.0) - 0.25 * scaled)

    def step_m():
        for r in parts:
            square = dot(mat_b[r, :], mat_b[...])
            sq_b[r, :] = square.astype(BF16)
            mat[r, :] = C0 * mat[r, :] + C1 * square
        for r in parts:
            cube = dot(mat_b[r, :], sq_b[...])
            mat[r, :] = mat[r, :] + C2 * cube
            mix_b[r, :] = (C3 * sq_b[r, :].astype(F32) + C4 * cube).astype(BF16)
        for r in parts:
            new = mat[r, :] + dot(sq_b[r, :], mix_b[...])
            mat[r, :] = new
            mat_b[r, :] = new.astype(BF16)

    def step_h(j, it):
        share = jnp.where(it < counts[j], 0.25, 0.0).astype(F32)
        for r in parts:
            held = mat_h[r, :]
            mat_h[r, :] = held + share * (held - dot(held.astype(BF16), mat_b[...]))

    def finish(j):
        share = jnp.where(ITERS - 1 < counts[j], 0.25, 0.0).astype(F32)
        for r in parts:
            held = mat_h[r, :]
            held = held + share * (held - dot(held.astype(BF16), mat_b[...]))
            root[j, r, :] = held.astype(BF16)

    def slab_copy(j, p):
        return pltpu.make_async_remote_copy(
            src_ref=root.at[j, pl.ds(pl.multiple_of((mp ^ p) * slab, slab), slab)],
            dst_ref=out.at[dp, mp, j],
            send_sem=sems["ssend"].at[j, p],
            recv_sem=sems["srecv"].at[j, p],
            device_id=peers[p],
            device_id_type=MESH,
        )

    slab_copies = [[p and slab_copy(j, p) for p in range(NP)] for j in range(2)]

    def piece(j, dy, dx, t):
        origin = lax.rem(dp + 4 * (NY - dy), NY * NX * NC) ^ (2 * dx)
        return out.at[origin, pl.ds(2 * ((mp // 2) ^ t), 2), j]

    def move(j, dy, dx, t, way):
        target = {"x": across, "+": up, "-": down, "s": sibling}[way]
        to_dy = {"x": dy, "+": (dy + 1) % NY, "-": (dy - 1) % NY, "s": dy}[way]
        to_dx = dx ^ 1 if way == "x" else dx
        side = "xys"["x+-s".index(way) if way == "x" else (2 if way == "s" else 1)]
        name = {"x": 0, "y": 0, "s": 1}[side]
        return pltpu.make_async_remote_copy(
            src_ref=piece(j, dy, dx, t),
            dst_ref=piece(j, dy, dx, t),
            send_sem=sems["bsend"].at[j, "x+-s".index(way), dy * 2 + dx, t],
            recv_sem=sems["brecv"].at[j, name, to_dy * 2 + to_dx, t],
            device_id=target,
            device_id_type=MESH,
        )

    started = []

    def send(j, dy, dx, t, ways):
        for way in ways:
            copy = move(j, dy, dx, t, way)
            copy.start()
            started.append(copy)

    def arrived(j, dy, dx, t, side=0):
        pltpu.make_async_remote_copy(
            src_ref=piece(j, dy, dx, t),
            dst_ref=piece(j, dy, dx, t),
            send_sem=sems["bsend"].at[j, 3, dy * 2 + dx, t],
            recv_sem=sems["brecv"].at[j, side, dy * 2 + dx, t],
            device_id=sibling,
            device_id_type=MESH,
        ).wait_recv()

    def spread(j):
        for p in range(1, NP):
            slab_copies[j][p].start()
        out[dp, mp, j] = root[j, pl.ds(pl.multiple_of(mp * slab, slab), slab), :]
        for t in range(NP // 2):
            for p in (2 * t, 2 * t + 1):
                if p:
                    slab_copies[j][p].wait_recv()
            send(j, 0, 0, t, ways_on(KINDS[j][t], 0, 0) + "s")

    relays = [arrival_order(KINDS[j]) for j in range(2)]

    def relay(j, first, last):
        for dy, dx, t in relays[j][first:last]:
            arrived(j, dy, dx, t)
            send(j, dy, dx, t, ways_on(KINDS[j][t], dy, dx) + "s")

    core = lax.rem(dp, NC)

    def take_turn(p):
        pl.semaphore_wait(sems["turn"].at[p], 1)

    def pass_turn(p):
        pl.semaphore_signal(sems["turn"].at[p], inc=1, device_id=sibling, device_id_type=MESH)

    for p in range(1, NP):
        pl.when(core == 1)(functools.partial(take_turn, p))
        grad_copies[0][p].start()
    mine[0].wait()
    add_gram(0, 0)
    for p in range(1, NP):
        grad_copies[0][p].wait_send()
        pass_turn(p)
    for p in range(1, NP):
        grad_copies[0][p].wait_recv()
        add_gram(0, p)
    tally.wait()
    update_stat(0)
    step_m()

    def body(it, _):
        step_h(0, it)
        step_m()
        return 0

    lax.fori_loop(1, ITERS - 1, body, 0)
    finish(0)

    spread(0)
    for p in range(1, NP):
        pl.when(core == 0)(functools.partial(take_turn, p))
        grad_copies[1][p].start()

    relay(0, 0, STOPS[0])
    relay(0, STOPS[0], STOPS[1])
    mine[1].wait()
    add_gram(1, 0)
    for p in range(1, NP):
        grad_copies[1][p].wait_send()
    for p in range(1, NP):
        grad_copies[1][p].wait_recv()
        add_gram(1, p)
    update_stat(1)
    step_m()
    for it in range(1, ITERS - 1):
        relay(0, STOPS[it], STOPS[it + 1])
        step_h(1, it)
        step_m()
    relay(0, STOPS[ITERS - 1], STOPS[ITERS])
    finish(1)
    spread(1)
    relay(0, STOPS[ITERS], len(relays[0]))
    relay(1, 0, len(relays[1]))

    for j in range(2):
        for dy in range(NY):
            for dx in range(NX):
                for t in range(4):
                    arrived(j, dy, dx, t, 1)
        for p in range(1, NP):
            slab_copies[j][p].wait_send()
    for copy in started:
        copy.wait_send()


def store(stat, out, stat_to, out_to, sems):
    size = out.shape[0] // STORES
    copies = [pltpu.make_async_copy(stat, stat_to, sems.at[STORES])]
    for k in range(STORES):
        span = pl.ds(k * size, size)
        copies.append(pltpu.make_async_copy(out.at[span], out_to.at[span], sems.at[k]))
    for copy in copies:
        copy.start()
    for copy in copies:
        copy.wait()


def solution(mesh):
    def step(grads, old_stat, counts):
        order = old_stat.shape[1]
        rows = grads.shape[1]
        slab = order // NP
        square = (order, order)
        sems = {
            "old": pltpu.SemaphoreType.DMA((2,)),
            "mine": pltpu.SemaphoreType.DMA((2,)),
            "count": pltpu.SemaphoreType.DMA(()),
            "turn": pltpu.SemaphoreType.REGULAR((NP,)),
            "gsend": pltpu.SemaphoreType.DMA((2, NP)),
            "grecv": pltpu.SemaphoreType.DMA((2, NP)),
            "ssend": pltpu.SemaphoreType.DMA((2, NP)),
            "srecv": pltpu.SemaphoreType.DMA((2, NP)),
            "bsend": pltpu.SemaphoreType.DMA((2, 4, NY * NX, 4)),
            "brecv": pltpu.SemaphoreType.DMA((2, 2, NY * NX, 4)),
        }
        stat, out = pl.pallas_call(
            kernel,
            out_shape=(
                pltpu.VMEM((2, order, order), F32),
                pltpu.VMEM((NY * NX * NC, NP, 2, slab, order), BF16),
            ),
            in_specs=[pl.BlockSpec(memory_space=pltpu.HBM)] * 3,
            out_specs=(pl.BlockSpec(memory_space=pltpu.VMEM), pl.BlockSpec(memory_space=pltpu.VMEM)),
            scratch_shapes=[
                pltpu.SMEM((2,), jnp.int32),
                pltpu.VMEM((2, NP * rows, order), BF16),
                pltpu.VMEM((2, order, order), F32),
                pltpu.VMEM((2, order, order), BF16),
                pltpu.VMEM(square, F32),
                pltpu.VMEM(square, BF16),
                pltpu.VMEM(square, BF16),
                pltpu.VMEM(square, BF16),
                pltpu.VMEM(square, F32),
                pltpu.VMEM(square, F32),
                sems,
            ],
            name="shampoo_roots",
            compiler_params=pltpu.CompilerParams(
                collective_id=0, has_side_effects=True, vmem_limit_bytes=24 * 2**20
            ),
        )(*(pltpu.with_memory_space_constraint(x, pltpu.HBM) for x in (grads, old_stat, counts)))
        out = out.reshape(NY * NX * NC * NP * 2, slab, order)
        anywhere = pl.BlockSpec(memory_space=pl.ANY)
        return pl.pallas_call(
            store,
            out_shape=(pltpu.HBM(stat.shape, F32), pltpu.HBM(out.shape, BF16)),
            in_specs=[pl.BlockSpec(memory_space=pltpu.VMEM)] * 2,
            out_specs=(pl.BlockSpec(memory_space=pltpu.HBM),) * 2,
            scratch_shapes=[pltpu.SemaphoreType.DMA((STORES + 1,))],
            name="store_results",
            compiler_params=pltpu.CompilerParams(vmem_limit_bytes=2**20),
        )(*(pltpu.with_memory_space_constraint(x, pltpu.VMEM) for x in (stat, out)))

    return jax.shard_map(
        step,
        mesh=mesh,
        in_specs=(P("dp", "mp", None), P(("dp", "mp"), None, None), P(("dp", "mp"))),
        out_specs=(P(("dp", "mp"), None, None), P(None, "mp", None)),
        check_vma=False,
    )
```

```python
import functools

import jax
import jax.numpy as jnp
from jax import lax
from jax.experimental import pallas as pl
from jax.experimental.pallas import tpu as pltpu
from jax.sharding import PartitionSpec as P

MESH = pl.DeviceIdType.MESH
F32, BF16 = jnp.float32, jnp.bfloat16
ITERS = 6
NY, NX, NC, NP = 4, 2, 2, 8
C0, C1, C2, C3, C4 = 1.25**4, -4 * 1.25**3 * 0.25, 6 * 1.25**2 * 0.25**2, -4 * 1.25 * 0.25**3, 0.25**4


STORES = 8
X, Y = "x", "y"
FULL = ((X, "+"), (X, "-"), (X, "+"), (X, "-"))
HALF = ((Y, "+"), (X, "+"), (X, "-"), (Y, "-"))
KINDS = (FULL, HALF)
STOPS = (4, 10, 12, 14, 16, 18, 20)


def ways_on(kind, dy, dx):
    first, far = kind
    near = "-" if far == "+" else "+"
    ways = ""
    if first == "x" and (dy, dx) == (0, 0):
        ways += "x"
    if first == "x" or dx == 0:
        if dy == 0:
            ways += far + near
        elif dy == (1 if far == "+" else NY - 1):
            ways += far
    if first == "y" and dx == 0:
        ways += "x"
    return ways


def arrival_order(kinds):
    free = {"x": 0.0, "+": 0.0, "-": 0.0}
    events = [(0.6 * t, 0, 0, t) for t in range(len(kinds))]
    order = []
    while events:
        events.sort()
        now, dy, dx, t = events.pop(0)
        if (dy, dx) != (0, 0):
            order.append((dy, dx, t))
        for way in ways_on(kinds[t], dy, dx):
            free[way] = max(free[way], now) + 1.0
            to_dy = (dy + {"x": 0, "+": 1, "-": -1}[way]) % NY
            events.append((free[way] + 1.0, to_dy, dx ^ 1 if way == "x" else dx, t))
    return order


def dot(left, right):
    return jnp.dot(left, right, preferred_element_type=F32)


def kernel(grads, old_hbm, counts_hbm, stat, out, counts, got, old, root, mat, mat_b, sq_b, mix_b, mat_h, acc, sems):
    order = old.shape[1]
    dp, mp = lax.axis_index("dp"), lax.axis_index("mp")
    rows = grads.shape[1]
    slab = order // NP
    chunk = order // 2
    parts = [slice(r, r + chunk) for r in range(0, order, chunk)]

    across = (dp ^ 2, mp)
    up = (lax.rem(dp + 4, NY * NX * NC), mp)
    down = (lax.rem(dp + 12, NY * NX * NC), mp)
    sibling = (dp ^ 1, mp)
    peers = [(dp, mp ^ p) for p in range(NP)]

    barrier = pltpu.get_barrier_semaphore()
    partners = peers[1:] + [across, up, down, sibling]
    for partner in partners:
        pl.semaphore_signal(barrier, inc=1, device_id=partner, device_id_type=MESH)

    keep = [pltpu.make_async_copy(old_hbm.at[j], old.at[j], sems["old"].at[j]) for j in range(2)]
    tally = pltpu.make_async_copy(counts_hbm, counts, sems["count"])
    tally.start()
    for copy in keep:
        copy.start()
    mine = [
        pltpu.make_async_copy(
            grads.at[2 * mp + j], got.at[j, pl.ds(mp * rows, rows)], sems["mine"].at[j]
        )
        for j in range(2)
    ]
    for copy in mine:
        copy.start()
    pl.semaphore_wait(barrier, len(partners))

    def grad_copy(j, p):
        return pltpu.make_async_remote_copy(
            src_ref=grads.at[2 * (mp ^ p) + j],
            dst_ref=got.at[j, pl.ds(mp * rows, rows)],
            send_sem=sems["gsend"].at[j, p],
            recv_sem=sems["grecv"].at[j, p],
            device_id=peers[p],
            device_id_type=MESH,
        )

    grad_copies = [[p and grad_copy(j, p) for p in range(NP)] for j in range(2)]

    def add_gram(j, p):
        block = got[j, pl.ds(pl.multiple_of((mp ^ p) * rows, rows), rows), :]
        gram = lax.dot_general(block, block, (((0,), (0,)), ((), ())), preferred_element_type=F32)
        if p == 0:
            acc[...] = gram
        else:
            acc[...] += gram

    def update_stat(j):
        keep[j].wait()
        total = jnp.zeros((1, order), F32)
        for r in parts:
            new = 0.95 * old[j, r, :] + 0.05 * acc[r, :]
            stat[j, r, :] = new
            total = total + jnp.sum(new * new, axis=0, keepdims=True)
        total = jnp.sum(total, axis=1, keepdims=True)
        zval = 2.5 / jnp.sqrt(total)
        start = jnp.sqrt(jnp.sqrt(zval))
        for r in parts:
            scaled = stat[j, r, :] * zval
            mat[r, :] = scaled
            mat_b[r, :] = scaled.astype(BF16)
            row = lax.broadcasted_iota(jnp.int32, (chunk, order), 0) + r.start
            col = lax.broadcasted_iota(jnp.int32, (chunk, order), 1)
            mat_h[r, :] = start * (jnp.where(row == col, 1.25, 0.0) - 0.25 * scaled)

    def step_m():
        for r in parts:
            square = dot(mat_b[r, :], mat_b[...])
            sq_b[r, :] = square.astype(BF16)
            mat[r, :] = C0 * mat[r, :] + C1 * square
        for r in parts:
            cube = dot(mat_b[r, :], sq_b[...])
            mat[r, :] = mat[r, :] + C2 * cube
            mix_b[r, :] = (C3 * sq_b[r, :].astype(F32) + C4 * cube).astype(BF16)
        for r in parts:
            new = mat[r, :] + dot(sq_b[r, :], mix_b[...])
            mat[r, :] = new
            mat_b[r, :] = new.astype(BF16)

    def step_h(j, it):
        share = jnp.where(it < counts[j], 0.25, 0.0).astype(F32)
        for r in parts:
            held = mat_h[r, :]
            mat_h[r, :] = held + share * (held - dot(held.astype(BF16), mat_b[...]))

    def finish(j):
        share = jnp.where(ITERS - 1 < counts[j], 0.25, 0.0).astype(F32)
        for r in parts:
            held = mat_h[r, :]
            held = held + share * (held - dot(held.astype(BF16), mat_b[...]))
            root[j, r, :] = held.astype(BF16)

    def slab_copy(j, p):
        return pltpu.make_async_remote_copy(
            src_ref=root.at[j, pl.ds(pl.multiple_of((mp ^ p) * slab, slab), slab)],
            dst_ref=out.at[dp, mp, j],
            send_sem=sems["ssend"].at[j, p],
            recv_sem=sems["srecv"].at[j, p],
            device_id=peers[p],
            device_id_type=MESH,
        )

    slab_copies = [[p and slab_copy(j, p) for p in range(NP)] for j in range(2)]

    def piece(j, dy, dx, t):
        origin = lax.rem(dp + 4 * (NY - dy), NY * NX * NC) ^ (2 * dx)
        return out.at[origin, pl.ds(2 * ((mp // 2) ^ t), 2), j]

    def move(j, dy, dx, t, way):
        target = {"x": across, "+": up, "-": down, "s": sibling}[way]
        to_dy = {"x": dy, "+": (dy + 1) % NY, "-": (dy - 1) % NY, "s": dy}[way]
        to_dx = dx ^ 1 if way == "x" else dx
        side = "xys"["x+-s".index(way) if way == "x" else (2 if way == "s" else 1)]
        name = {"x": 0, "y": 0, "s": 1}[side]
        return pltpu.make_async_remote_copy(
            src_ref=piece(j, dy, dx, t),
            dst_ref=piece(j, dy, dx, t),
            send_sem=sems["bsend"].at[j, "x+-s".index(way), dy * 2 + dx, t],
            recv_sem=sems["brecv"].at[j, name, to_dy * 2 + to_dx, t],
            device_id=target,
            device_id_type=MESH,
        )

    started = []

    def send(j, dy, dx, t, ways):
        for way in ways:
            copy = move(j, dy, dx, t, way)
            copy.start()
            started.append(copy)

    def arrived(j, dy, dx, t, side=0):
        pltpu.make_async_remote_copy(
            src_ref=piece(j, dy, dx, t),
            dst_ref=piece(j, dy, dx, t),
            send_sem=sems["bsend"].at[j, 3, dy * 2 + dx, t],
            recv_sem=sems["brecv"].at[j, side, dy * 2 + dx, t],
            device_id=sibling,
            device_id_type=MESH,
        ).wait_recv()

    def spread(j, meanwhile=0):
        for p in range(1, NP):
            slab_copies[j][p].start()
        if meanwhile:
            relay(0, meanwhile, len(relays[0]))
        out[dp, mp, j] = root[j, pl.ds(pl.multiple_of(mp * slab, slab), slab), :]
        for t in range(NP // 2):
            for p in (2 * t, 2 * t + 1):
                if p:
                    slab_copies[j][p].wait_recv()
            send(j, 0, 0, t, ways_on(KINDS[j][t], 0, 0) + "s")

    relays = [arrival_order(KINDS[j]) for j in range(2)]

    def relay(j, first, last):
        for dy, dx, t in relays[j][first:last]:
            arrived(j, dy, dx, t)
            send(j, dy, dx, t, ways_on(KINDS[j][t], dy, dx) + "s")

    core = lax.rem(dp, NC)

    def take_turn(p):
        pl.semaphore_wait(sems["turn"].at[p], 1)

    def pass_turn(p):
        pl.semaphore_signal(sems["turn"].at[p], inc=1, device_id=sibling, device_id_type=MESH)

    for p in range(1, NP):
        pl.when(core == 1)(functools.partial(take_turn, p))
        grad_copies[0][p].start()
    mine[0].wait()
    add_gram(0, 0)
    for p in range(1, NP):
        grad_copies[0][p].wait_send()
        pass_turn(p)
    for p in range(1, NP):
        grad_copies[0][p].wait_recv()
        add_gram(0, p)
    tally.wait()
    update_stat(0)
    step_m()

    def body(it, _):
        step_h(0, it)
        step_m()
        return 0

    lax.fori_loop(1, ITERS - 1, body, 0)
    finish(0)

    spread(0)
    for p in range(1, NP):
        pl.when(core == 0)(functools.partial(take_turn, p))
        grad_copies[1][p].start()

    relay(0, 0, STOPS[0])
    relay(0, STOPS[0], STOPS[1])
    mine[1].wait()
    add_gram(1, 0)
    for p in range(1, NP):
        grad_copies[1][p].wait_send()
    for p in range(1, NP):
        grad_copies[1][p].wait_recv()
        add_gram(1, p)
    update_stat(1)
    step_m()
    for it in range(1, ITERS - 1):
        relay(0, STOPS[it], STOPS[it + 1])
        step_h(1, it)
        step_m()
    relay(0, STOPS[ITERS - 1], STOPS[ITERS])
    finish(1)
    spread(1, STOPS[ITERS])
    relay(1, 0, len(relays[1]))

    for j in range(2):
        for dy in range(NY):
            for dx in range(NX):
                for t in range(4):
                    arrived(j, dy, dx, t, 1)
        for p in range(1, NP):
            slab_copies[j][p].wait_send()
    for copy in started:
        copy.wait_send()


def store(stat, out, stat_to, out_to, sems):
    size = out.shape[0] // STORES
    copies = [pltpu.make_async_copy(stat, stat_to, sems.at[STORES])]
    for k in range(STORES):
        span = pl.ds(k * size, size)
        copies.append(pltpu.make_async_copy(out.at[span], out_to.at[span], sems.at[k]))
    for copy in copies:
        copy.start()
    for copy in copies:
        copy.wait()


def solution(mesh):
    def step(grads, old_stat, counts):
        order = old_stat.shape[1]
        rows = grads.shape[1]
        slab = order // NP
        square = (order, order)
        sems = {
            "old": pltpu.SemaphoreType.DMA((2,)),
            "mine": pltpu.SemaphoreType.DMA((2,)),
            "count": pltpu.SemaphoreType.DMA(()),
            "turn": pltpu.SemaphoreType.REGULAR((NP,)),
            "gsend": pltpu.SemaphoreType.DMA((2, NP)),
            "grecv": pltpu.SemaphoreType.DMA((2, NP)),
            "ssend": pltpu.SemaphoreType.DMA((2, NP)),
            "srecv": pltpu.SemaphoreType.DMA((2, NP)),
            "bsend": pltpu.SemaphoreType.DMA((2, 4, NY * NX, 4)),
            "brecv": pltpu.SemaphoreType.DMA((2, 2, NY * NX, 4)),
        }
        stat, out = pl.pallas_call(
            kernel,
            out_shape=(
                pltpu.VMEM((2, order, order), F32),
                pltpu.VMEM((NY * NX * NC, NP, 2, slab, order), BF16),
            ),
            in_specs=[pl.BlockSpec(memory_space=pltpu.HBM)] * 3,
            out_specs=(pl.BlockSpec(memory_space=pltpu.VMEM), pl.BlockSpec(memory_space=pltpu.VMEM)),
            scratch_shapes=[
                pltpu.SMEM((2,), jnp.int32),
                pltpu.VMEM((2, NP * rows, order), BF16),
                pltpu.VMEM((2, order, order), F32),
                pltpu.VMEM((2, order, order), BF16),
                pltpu.VMEM(square, F32),
                pltpu.VMEM(square, BF16),
                pltpu.VMEM(square, BF16),
                pltpu.VMEM(square, BF16),
                pltpu.VMEM(square, F32),
                pltpu.VMEM(square, F32),
                sems,
            ],
            name="shampoo_roots",
            compiler_params=pltpu.CompilerParams(
                collective_id=0, has_side_effects=True, vmem_limit_bytes=24 * 2**20
            ),
        )(*(pltpu.with_memory_space_constraint(x, pltpu.HBM) for x in (grads, old_stat, counts)))
        out = out.reshape(NY * NX * NC * NP * 2, slab, order)
        anywhere = pl.BlockSpec(memory_space=pl.ANY)
        return pl.pallas_call(
            store,
            out_shape=(pltpu.HBM(stat.shape, F32), pltpu.HBM(out.shape, BF16)),
            in_specs=[pl.BlockSpec(memory_space=pltpu.VMEM)] * 2,
            out_specs=(pl.BlockSpec(memory_space=pltpu.HBM),) * 2,
            scratch_shapes=[pltpu.SemaphoreType.DMA((STORES + 1,))],
            name="store_results",
            compiler_params=pltpu.CompilerParams(vmem_limit_bytes=2**20),
        )(*(pltpu.with_memory_space_constraint(x, pltpu.VMEM) for x in (stat, out)))

    return jax.shard_map(
        step,
        mesh=mesh,
        in_specs=(P("dp", "mp", None), P(("dp", "mp"), None, None), P(("dp", "mp"))),
        out_specs=(P(("dp", "mp"), None, None), P(None, "mp", None)),
        check_vma=False,
    )
```
